32 devices in a mesh: groups: 2 (over x), yslab: 16 (over z, y, core).
Axes of the slice: x: 2, y: 2, z: 4, core: 2. Of those that a mesh axis runs over, the one named last changes fastest.
Arguments:
- signal: bfloat16 [20, 64, 64, 128], P(None, 'groups', 'yslab'), parts along dimension 1, may hold values from -6 to 6
- cotangent: bfloat16 [20, 64, 64, 128], P(None, 'groups', 'yslab'), parts along dimension 1, may hold values from -6 to 6
- spectral_weight: bfloat16 [512, 25600], P('yslab'), may hold values from -1.25 to 1.25
- mix_weight: float32 [20, 20], replicated, may hold values from -1.25 to 1.25
- mix_bias: float32 [20], replicated, may hold values from -3 to 3
Outputs:
- activation: bfloat16 [20, 64, 64, 128], P(None, 'groups', 'yslab'), parts along dimension 1
- grad_input: bfloat16 [20, 64, 64, 128], P(None, 'groups', 'yslab'), parts along dimension 1
- grad_spectral: float32 [512, 51200], P('yslab', 'groups'), parts along dimension 1
- grad_mix: float32 [40, 20], P('groups'), parts along dimension 0
- grad_bias: float32 [40], P('groups'), parts along dimension 0
The draws below stay inside these ranges and needn't reach their ends.
There are 2 independent parts, one for each index of `groups`. The reference program is written for one: setup_inputs(seed, part) draws one part's arguments, and reference() takes and returns one part's arrays. A program takes and returns all parts, laid end to end along the dimension named above; an argument that names none is the same for every part. Nothing has to cross between parts.
All inputs are finite; a program needn't handle non-finite values.
Results may differ from the reference program's by a relative error of at most 0.001.
Values sent between devices are 32-bit elements; how exact they have to be, the bound alone decides.
A program may use at most 128 MiB of HBM per device.

```python
import math
import jax
import jax.numpy as jnp
from jax import lax

C = 20
MODES = 16
NX = 32
NZ = 128
NY = 64
PAIRS = 512


def steps_of(stream_key, extent, pieces, low, high):
    level, own = 1.0, jax.random.fold_in(stream_key, 6)
    for dim, blocks in pieces:
        steps = jnp.exp(jax.random.uniform(jax.random.fold_in(own, dim), (blocks,), jnp.float32, low / len(pieces), high / len(pieces)))
        level = level * jnp.repeat(steps, extent[dim] // blocks).reshape([-1 if axis == dim else 1 for axis in range(len(extent))])
    return level


def gaussian(stream_key, extent, spread, reach, cuts=(), kind=jnp.bfloat16):
    entries = jax.random.normal(stream_key, extent, jnp.float32) * spread
    if len(cuts) > 0:
        entries = steps_of(stream_key, extent, cuts, -0.22, 0.18) * entries
    return jnp.clip(entries, min=-reach, max=reach).astype(kind)


def setup_inputs(seed: int = 0, part: int = 0) -> dict:
    keys = jax.random.split(jax.random.key(seed), 6)
    part_splits = jax.random.split(jax.random.fold_in(keys[5], part), 6)
    return {
        "signal": gaussian(part_splits[0], (C, NX, NY, NZ), 1.0, 6.0, ((2, 16),)),
        "cotangent": gaussian(part_splits[1], (C, NX, NY, NZ), 1.0, 6.0, ((2, 16),)),
        "spectral_weight": gaussian(keys[2], (PAIRS, 2 * C * C * 2 * MODES), C ** -0.5, 1.25, ((0, 16),)),
        "mix_weight": gaussian(keys[3], (C, C), C ** -0.5, 1.25, (), jnp.float32),
        "mix_bias": gaussian(keys[4], (C,), 0.5, 3.0, (), jnp.float32),
    }


def contract(form, left, right):
    return jnp.einsum(form, left, right, precision=lax.Precision.HIGHEST)

def signed_waves(modes):
    return jnp.concatenate([jnp.arange(modes, dtype=jnp.int32), jnp.arange(-modes, 0, dtype=jnp.int32)])

def tables(places, length, wavenum):
    phase = jnp.mod(places[:, None] * wavenum[None, :], length).astype(jnp.float32)
    angle = phase * (2.0 * math.pi / length)
    return (jnp.cos(angle), jnp.sin(angle))

def all_tables():
    waves = signed_waves(MODES)
    cos_x, sin_x = tables(jnp.arange(NX, dtype=jnp.int32), NX, waves)
    cos_y, sin_y = tables(jnp.arange(NY, dtype=jnp.int32), NY, waves)
    cos_z, sin_z = tables(jnp.arange(NZ, dtype=jnp.int32), NZ, jnp.arange(MODES, dtype=jnp.int32))
    return (cos_x, sin_x, cos_y, sin_y, cos_z, sin_z)

def forward_modes(field, scale):
    cos_x, sin_x, cos_y, sin_y, cos_z, sin_z = all_tables()
    first_re = contract('cxyz,zk->cxyk', field, cos_z)
    first_im = -contract('cxyz,zk->cxyk', field, sin_z)
    second_re = contract('cxyk,xj->cjyk', first_re, cos_x) + contract('cxyk,xj->cjyk', first_im, sin_x)
    second_im = contract('cxyk,xj->cjyk', first_im, cos_x) - contract('cxyk,xj->cjyk', first_re, sin_x)
    third_re = contract('cjyk,ym->cjkm', second_re, cos_y) + contract('cjyk,ym->cjkm', second_im, sin_y)
    third_im = contract('cjyk,ym->cjkm', second_im, cos_y) - contract('cjyk,ym->cjkm', second_re, sin_y)
    shape = (C, PAIRS, 2 * MODES)
    return (scale * third_re.reshape(shape), scale * third_im.reshape(shape))

def inverse_modes(spec_re, spec_im, scale):
    cos_x, sin_x, cos_y, sin_y, cos_z, sin_z = all_tables()
    shape = (C, 2 * MODES, MODES, 2 * MODES)
    spec_re = spec_re.reshape(shape)
    spec_im = spec_im.reshape(shape)
    first_re = contract('cjkm,ym->cjyk', spec_re, cos_y) - contract('cjkm,ym->cjyk', spec_im, sin_y)
    first_im = contract('cjkm,ym->cjyk', spec_im, cos_y) + contract('cjkm,ym->cjyk', spec_re, sin_y)
    second_re = contract('cjyk,xj->cxyk', first_re, cos_x) - contract('cjyk,xj->cxyk', first_im, sin_x)
    second_im = contract('cjyk,xj->cxyk', first_im, cos_x) + contract('cjyk,xj->cxyk', first_re, sin_x)
    field = contract('cxyk,zk->cxyz', second_re, cos_z) - contract('cxyk,zk->cxyz', second_im, sin_z)
    return scale * field

def layer(field, weights, mixing, bias):
    scale_fwd = 1.0 / math.sqrt(NX * NY * NZ)
    scale_inv = 1.0 / math.sqrt(4 * MODES ** 3)
    modes_re, modes_im = forward_modes(field, scale_fwd)
    w_real = weights[:, 0]
    w_imag = weights[:, 1]
    mixed_re = contract('pcom,cpm->opm', w_real, modes_re) - contract('pcom,cpm->opm', w_imag, modes_im)
    mixed_im = contract('pcom,cpm->opm', w_real, modes_im) + contract('pcom,cpm->opm', w_imag, modes_re)
    spectral = inverse_modes(mixed_re, mixed_im, scale_inv)
    pre = spectral + contract('cxyz,co->oxyz', field, mixing) + bias[:, None, None, None]
    return jax.nn.gelu(pre, approximate=True)

def reference(signal, cotangent, spectral_weight, mix_weight, mix_bias):
    field = signal.astype(jnp.float32)
    weights = spectral_weight.astype(jnp.float32).reshape(PAIRS, 2, C, C, 2 * MODES)
    result, pullback = jax.vjp(layer, field, weights, mix_weight, mix_bias)
    grads = pullback(cotangent.astype(jnp.float32))
    norm_scale = 1.0 / math.sqrt(NX * NY * NZ)
    activation = result.astype(jnp.bfloat16)
    grad_input = grads[0].astype(jnp.bfloat16)
    grad_spectral = grads[1].reshape(PAIRS, 2 * C * C * 2 * MODES)
    return (activation, grad_input, grad_spectral, grads[2] * norm_scale, grads[3] * norm_scale)
```

```python
from functools import partial
import math

import jax
import jax.numpy as jnp
from jax import lax
from jax.sharding import PartitionSpec as P

MODES = 16
PAIRS = 512


def contract(form, left, right):
    return jnp.einsum(
        form, left, right, precision=lax.Precision.HIGH, preferred_element_type=jnp.float32
    )


def signed_waves(modes):
    return jnp.concatenate(
        [jnp.arange(modes, dtype=jnp.int32), jnp.arange(-modes, 0, dtype=jnp.int32)]
    )


def tables(places, length, wavenum):
    phase = jnp.mod(places[:, None] * wavenum[None, :], length).astype(jnp.float32)
    angle = phase * (2.0 * math.pi / length)
    return (jnp.cos(angle), jnp.sin(angle))


def per_device(signal, cotangent, spectral_weight, mix_weight, mix_bias):
    channels, width_x, rows_y, width_z = signal.shape
    slabs = lax.axis_size("yslab")
    length_y = rows_y * slabs
    waves = signed_waves(MODES)
    cos_x, sin_x = tables(jnp.arange(width_x, dtype=jnp.int32), width_x, waves)
    cos_z, sin_z = tables(
        jnp.arange(width_z, dtype=jnp.int32), width_z, jnp.arange(MODES, dtype=jnp.int32)
    )
    scale_fwd = 1.0 / math.sqrt(width_x * length_y * width_z)
    scale_inv = 1.0 / math.sqrt(4 * MODES**3)

    all_rows = jnp.arange(length_y, dtype=jnp.int32)
    cos_y, sin_y = tables(all_rows, length_y, waves)
    turn_y = jnp.stack(
        [jnp.stack([cos_y, -sin_y], axis=1), jnp.stack([sin_y, cos_y], axis=1)]
    ).reshape(2, slabs, rows_y, 2, 2 * MODES)
    owned = PAIRS // slabs
    back_x = jnp.stack([jnp.stack([cos_x, sin_x]), jnp.stack([-sin_x, cos_x])])
    turn_z = jnp.stack([cos_z, -sin_z])

    def to_modes(field, scale):
        first = contract("cxyz,rzk->rcxyk", field, turn_z)
        second = contract(
            "rcxyk,rqxj->qcyjk", first, jnp.stack(
                [jnp.stack([cos_x, -sin_x]), jnp.stack([sin_x, cos_x])]
            )
        )
        blocks = second.reshape(2, channels, rows_y, slabs, owned)
        blocks = jnp.transpose(blocks, (3, 0, 2, 1, 4))
        rows = lax.all_to_all(blocks, "yslab", split_axis=0, concat_axis=0, tiled=True)
        return contract("sqycp,qsyrm->prcm", rows, turn_y) * scale

    def to_grid(spectrum, scale):
        rows = contract("prcm,rsyqm->sqycp", spectrum, jnp.transpose(turn_y, (3, 1, 2, 0, 4)))
        rows = lax.all_to_all(rows, "yslab", split_axis=0, concat_axis=0, tiled=True)
        shaped = jnp.transpose(rows, (1, 3, 2, 0, 4)).reshape(
            2, channels, rows_y, 2 * MODES, MODES
        )
        second = contract("qcyjk,qrxj->rcxyk", shaped, back_x)
        return contract("rcxyk,rzk->cxyz", second, turn_z) * scale

    weights = spectral_weight.astype(jnp.float32).reshape(-1, 2, channels, channels, 2 * MODES)
    w_real = weights[:, 0]
    w_imag = weights[:, 1]
    spectrum = to_modes(signal, scale_fwd)
    modes_re = spectrum[:, 0]
    modes_im = spectrum[:, 1]
    mixed_re = contract("pcom,pcm->pom", w_real, modes_re) - contract(
        "pcom,pcm->pom", w_imag, modes_im
    )
    mixed_im = contract("pcom,pcm->pom", w_real, modes_im) + contract(
        "pcom,pcm->pom", w_imag, modes_re
    )
    spectral = to_grid(jnp.stack([mixed_re, mixed_im], axis=1), scale_inv)
    pre = spectral + contract("cxyz,co->oxyz", signal, mix_weight) + mix_bias[:, None, None, None]
    result, pullback = jax.vjp(partial(jax.nn.gelu, approximate=True), pre)
    activation = result.astype(jnp.bfloat16)
    dpre = pullback(cotangent.astype(jnp.float32))[0]
    dmixed = to_modes(dpre, scale_inv)
    dmixed_re = dmixed[:, 0]
    dmixed_im = dmixed[:, 1]
    dweight_re = contract("pcm,pom->pcom", modes_re, dmixed_re) + contract(
        "pcm,pom->pcom", modes_im, dmixed_im
    )
    dweight_im = contract("pcm,pom->pcom", modes_re, dmixed_im) - contract(
        "pcm,pom->pcom", modes_im, dmixed_re
    )
    grad_spectral = jnp.stack([dweight_re, dweight_im], axis=1).reshape(
        spectral_weight.shape[0], -1
    )
    dmodes_re = contract("pcom,pom->pcm", w_real, dmixed_re) + contract(
        "pcom,pom->pcm", w_imag, dmixed_im
    )
    dmodes_im = contract("pcom,pom->pcm", w_real, dmixed_im) - contract(
        "pcom,pom->pcm", w_imag, dmixed_re
    )
    back_field = to_grid(jnp.stack([dmodes_re, dmodes_im], axis=1), scale_fwd)
    grad_input = (back_field + contract("oxyz,co->cxyz", dpre, mix_weight)).astype(jnp.bfloat16)
    mix_sum, bias_sum = lax.psum(
        (contract("cxyz,oxyz->co", signal, dpre), jnp.sum(dpre, axis=(1, 2, 3))), "yslab"
    )
    return (activation, grad_input, grad_spectral, mix_sum * scale_fwd, bias_sum * scale_fwd)


def solution(mesh):
    placed = (
        P(None, "groups", "yslab", None),
        P(None, "groups", "yslab", None),
        P("yslab", None),
        P(),
        P(),
    )
    return jax.shard_map(
        per_device,
        mesh=mesh,
        in_specs=placed,
        out_specs=(
            P(None, "groups", "yslab", None),
            P(None, "groups", "yslab", None),
            P("yslab", "groups"),
            P("groups", None),
            P("groups"),
        ),
        check_vma=False,
    )
```

```python
from functools import partial
import math

import ml_dtypes
import numpy as np

import jax
import jax.numpy as jnp
from jax import lax
from jax.experimental import pallas as pl
from jax.experimental.pallas import tpu as pltpu
from jax.sharding import PartitionSpec as P

MODES = 16
PAIRS = 512


def contract(form, left, right):
    return jnp.einsum(
        form, left, right, precision=lax.Precision.HIGH, preferred_element_type=jnp.float32
    )


def signed_waves(modes):
    return jnp.concatenate(
        [jnp.arange(modes, dtype=jnp.int32), jnp.arange(-modes, 0, dtype=jnp.int32)]
    )


def tables(places, length, wavenum):
    phase = jnp.mod(places[:, None] * wavenum[None, :], length).astype(jnp.float32)
    angle = phase * (2.0 * math.pi / length)
    return (jnp.cos(angle), jnp.sin(angle))


def per_device_general(signal, cotangent, spectral_weight, mix_weight, mix_bias):
    channels, width_x, rows_y, width_z = signal.shape
    slabs = lax.axis_size("yslab")
    length_y = rows_y * slabs
    waves = signed_waves(MODES)
    cos_x, sin_x = tables(jnp.arange(width_x, dtype=jnp.int32), width_x, waves)
    cos_z, sin_z = tables(
        jnp.arange(width_z, dtype=jnp.int32), width_z, jnp.arange(MODES, dtype=jnp.int32)
    )
    scale_fwd = 1.0 / math.sqrt(width_x * length_y * width_z)
    scale_inv = 1.0 / math.sqrt(4 * MODES**3)

    all_rows = jnp.arange(length_y, dtype=jnp.int32)
    cos_y, sin_y = tables(all_rows, length_y, waves)
    turn_y = jnp.stack(
        [jnp.stack([cos_y, -sin_y], axis=1), jnp.stack([sin_y, cos_y], axis=1)]
    ).reshape(2, slabs, rows_y, 2, 2 * MODES)
    owned = PAIRS // slabs
    back_x = jnp.stack([jnp.stack([cos_x, sin_x]), jnp.stack([-sin_x, cos_x])])
    turn_z = jnp.stack([cos_z, -sin_z])

    def to_modes(field, scale):
        first = contract("cxyz,rzk->rcxyk", field, turn_z)
        second = contract(
            "rcxyk,rqxj->qcyjk", first, jnp.stack(
                [jnp.stack([cos_x, -sin_x]), jnp.stack([sin_x, cos_x])]
            )
        )
        blocks = second.reshape(2, channels, rows_y, slabs, owned)
        blocks = jnp.transpose(blocks, (3, 0, 2, 1, 4))
        rows = lax.all_to_all(blocks, "yslab", split_axis=0, concat_axis=0, tiled=True)
        return contract("sqycp,qsyrm->prcm", rows, turn_y) * scale

    def to_grid(spectrum, scale):
        rows = contract("prcm,rsyqm->sqycp", spectrum, jnp.transpose(turn_y, (3, 1, 2, 0, 4)))
        rows = lax.all_to_all(rows, "yslab", split_axis=0, concat_axis=0, tiled=True)
        shaped = jnp.transpose(rows, (1, 3, 2, 0, 4)).reshape(
            2, channels, rows_y, 2 * MODES, MODES
        )
        second = contract("qcyjk,qrxj->rcxyk", shaped, back_x)
        return contract("rcxyk,rzk->cxyz", second, turn_z) * scale

    weights = spectral_weight.astype(jnp.float32).reshape(-1, 2, channels, channels, 2 * MODES)
    w_real = weights[:, 0]
    w_imag = weights[:, 1]
    spectrum = to_modes(signal, scale_fwd)
    modes_re = spectrum[:, 0]
    modes_im = spectrum[:, 1]
    mixed_re = contract("pcom,pcm->pom", w_real, modes_re) - contract(
        "pcom,pcm->pom", w_imag, modes_im
    )
    mixed_im = contract("pcom,pcm->pom", w_real, modes_im) + contract(
        "pcom,pcm->pom", w_imag, modes_re
    )
    spectral = to_grid(jnp.stack([mixed_re, mixed_im], axis=1), scale_inv)
    pre = spectral + contract("cxyz,co->oxyz", signal, mix_weight) + mix_bias[:, None, None, None]
    result, pullback = jax.vjp(partial(jax.nn.gelu, approximate=True), pre)
    activation = result.astype(jnp.bfloat16)
    dpre = pullback(cotangent.astype(jnp.float32))[0]
    dmixed = to_modes(dpre, scale_inv)
    dmixed_re = dmixed[:, 0]
    dmixed_im = dmixed[:, 1]
    dweight_re = contract("pcm,pom->pcom", modes_re, dmixed_re) + contract(
        "pcm,pom->pcom", modes_im, dmixed_im
    )
    dweight_im = contract("pcm,pom->pcom", modes_re, dmixed_im) - contract(
        "pcm,pom->pcom", modes_im, dmixed_re
    )
    grad_spectral = jnp.stack([dweight_re, dweight_im], axis=1).reshape(
        spectral_weight.shape[0], -1
    )
    dmodes_re = contract("pcom,pom->pcm", w_real, dmixed_re) + contract(
        "pcom,pom->pcm", w_imag, dmixed_im
    )
    dmodes_im = contract("pcom,pom->pcm", w_real, dmixed_im) - contract(
        "pcom,pom->pcm", w_imag, dmixed_re
    )
    back_field = to_grid(jnp.stack([dmodes_re, dmodes_im], axis=1), scale_fwd)
    grad_input = (back_field + contract("oxyz,co->cxyz", dpre, mix_weight)).astype(jnp.bfloat16)
    mix_sum, bias_sum = lax.psum(
        (contract("cxyz,oxyz->co", signal, dpre), jnp.sum(dpre, axis=(1, 2, 3))), "yslab"
    )
    return (activation, grad_input, grad_spectral, mix_sum * scale_fwd, bias_sum * scale_fwd)


SLABS = 16
ROWS = 4
F32 = jnp.float32
BF16 = jnp.bfloat16
CHANS = [[oq * 4 + 2 * q + ii for ii in range(2) for oq in range(4)] for q in range(2)]
CHANS.append([16, 17, 18, 19])
CHUNKS = [(0, 2), (2, 2), (4, 1)]


def split_table(table):
    high = table.astype(ml_dtypes.bfloat16)
    low = (table - high.astype(np.float64)).astype(ml_dtypes.bfloat16)
    return np.stack([high, low])


def host_waves(places, length, wavenum):
    angle = np.mod(np.outer(places, wavenum), length) * (2.0 * math.pi / length)
    return np.cos(angle), np.sin(angle)


def host_tables(width_x, length_y, width_z):
    waves = np.concatenate([np.arange(MODES), np.arange(-MODES, 0)])
    cx, sx = host_waves(np.arange(width_x), width_x, waves)
    cy, sy = host_waves(np.arange(length_y), length_y, waves)
    cz, sz = host_waves(np.arange(width_z), width_z, np.arange(MODES))
    eye_y = np.eye(ROWS)
    fz = np.stack([cz, -sz])
    z8 = np.einsum("ab,rzk->azrbk", np.eye(8), fz).reshape(8 * width_z, 256)
    z4 = np.einsum("ab,rzk,e->azrebk", np.eye(4), fz, np.ones(2)).reshape(4 * width_z, 256)
    fx = np.stack([np.stack([cx, -sx]), np.stack([sx, cx])])
    wx = np.einsum("rqxdl,yt->ldyqrxt", fx.reshape(2, 2, width_x, SLABS, 2), eye_y)
    wx = wx.reshape(256, 256)
    bx = np.stack([np.stack([cx, sx]), np.stack([-sx, cx])])
    wxi = np.einsum("qrxdl,yt->rxtldyq", bx.reshape(2, 2, width_x, SLABS, 2), eye_y)
    wxi = wxi.reshape(256, 256)
    fy = np.stack([np.stack([cy, -sy]), np.stack([sy, cy])])
    ty = np.einsum("rqym,e->yrqem", fy, np.ones(4)).reshape(128, 256)
    by = np.stack([np.stack([cy, sy]), np.stack([-sy, cy])])
    tyi = np.einsum("rqym,ie->iyqrem", by, np.eye(4)).reshape(512, 256)
    tyr = np.einsum("rqym,e->yqrem", by, np.ones(4)).reshape(128, 256)
    zi8 = np.einsum("ab,rzk->rakbz", np.eye(8), fz).reshape(256, 8 * width_z)
    pick = np.stack([np.ones(1), np.zeros(1)]).reshape(2)
    zi4 = np.einsum("ab,rzk,e->raekbz", np.eye(4), fz, pick).reshape(256, 4 * width_z)
    return [split_table(t) for t in (z8, z4, wx, wxi, ty, tyi, tyr, zi8, zi4)]


def halves(value):
    high = value.astype(BF16)
    return high, (value - high.astype(F32)).astype(BF16)


def product(left, right, form=((1,), (0,))):
    def one(a, b):
        return lax.dot_general(a, b, (form, ((), ())), preferred_element_type=F32)

    total = one(left[0], right[0])
    if left[1] is not None:
        total = total + one(left[1], right[0])
    if right[1] is not None:
        total = total + one(left[0], right[1])
    return total


def block_kernel(scale_fwd, scale_inv, sig, cot, w, mix, bias, z8, z4, wx, wxi, ty, tyi, tyr, zi8,
                 zi4, act, gin, gspec, gsum, sf, point, dpre, modes, dmodes, spec, dspec, gmix,
                 send, recv, sums, send_sem, recv_sem, sum_send, sum_recv):
    me = lax.axis_index("yslab")
    channels = 20
    lane = lax.broadcasted_iota(jnp.int32, (128, 128), 1)

    def both(ref):
        return ref[0], ref[1]

    def copy(step, chunk, peer):
        first, count = CHUNKS[chunk]
        return pltpu.make_async_remote_copy(
            src_ref=send.at[step, peer, pl.ds(first, count)],
            dst_ref=recv.at[step, me, pl.ds(first, count)],
            send_sem=send_sem.at[step, chunk, peer],
            recv_sem=recv_sem.at[step, chunk, me],
            device_id={"yslab": peer},
            device_id_type=pl.DeviceIdType.MESH,
        )

    def arrival(step, chunk, peer):
        first, count = CHUNKS[chunk]
        return pltpu.make_async_remote_copy(
            src_ref=send.at[step, peer, pl.ds(first, count)],
            dst_ref=recv.at[step, peer, pl.ds(first, count)],
            send_sem=send_sem.at[step, chunk, peer],
            recv_sem=recv_sem.at[step, chunk, peer],
            device_id={"yslab": peer},
            device_id_type=pl.DeviceIdType.MESH,
        )

    def sum_copy(peer, source):
        return pltpu.make_async_remote_copy(
            src_ref=sums.at[me],
            dst_ref=sums.at[source],
            send_sem=sum_send.at[peer],
            recv_sem=sum_recv.at[source],
            device_id={"yslab": peer},
            device_id_type=pl.DeviceIdType.MESH,
        )

    def each_peer(action):
        def body(i, carry):
            action(lax.rem(me + i, SLABS))
            return carry

        lax.fori_loop(1, SLABS, body, 0)

    def send_chunk(step, chunk):
        each_peer(lambda peer: copy(step, chunk, peer).start())
        first, count = CHUNKS[chunk]
        recv[step, pl.ds(me, 1), first:first + count] = send[step, pl.ds(me, 1), first:first + count]

    def wait_chunk(step, chunk):
        each_peer(lambda peer: arrival(step, chunk, peer).wait_recv())

    def forward_group(step, group, read, exact):
        table = z8 if group < 2 else z4
        total = None
        for at in range(0, len(CHANS[group]), 2):
            pair = jnp.concatenate([read(c) for c in CHANS[group][at:at + 2]], axis=1)
            left = (pair, None) if exact else halves(pair)
            rows = slice(at * 128, at * 128 + 256)
            part = product(left, (table[0, rows], table[1, rows]))
            total = part if total is None else total + part
        stacked = jnp.concatenate([total[:, :128], total[:, 128:]], axis=0)
        out = product(both(wx), halves(stacked))
        if group < 2:
            for jl in range(2):
                send[step, :, 2 * group + jl] = out[jl * 128:(jl + 1) * 128].reshape(16, 8, 128)
        else:
            send[step, :, 4] = jnp.where(lane < 64, out[:128], out[128:]).reshape(16, 8, 128)
        send_chunk(step, group)

    def spectra(step, group, target, scale):
        for jl in range(2 if group < 2 else 1):
            tile = recv[step, :, 2 * group + jl].reshape(128, 128) * scale
            out = product(halves(tile.T), both(ty))
            if group < 2:
                for place, c in enumerate(CHANS[group]):
                    target[jl, c] = out[place * 16:(place + 1) * 16]
            else:
                for jj in range(2):
                    for place, c in enumerate(CHANS[2]):
                        row = jj * 64 + place * 16
                        target[jj, c] = out[row:row + 16]

    def back_group(step, group, use):
        if group < 2:
            one = recv[step, :, 2 * group].reshape(128, 128)
            two = recv[step, :, 2 * group + 1].reshape(128, 128)
            top = jnp.where(lane < 64, one, pltpu.roll(two, 64, 1))
            low = jnp.where(lane < 64, pltpu.roll(one, 64, 1), two)
        else:
            top = recv[step, :, 4].reshape(128, 128)
            low = pltpu.roll(top, 112, 1)
        out = product(both(wxi), halves(jnp.concatenate([top, low], axis=0)))
        left = halves(jnp.concatenate([out[:128], out[128:]], axis=1))
        table = zi8 if group < 2 else zi4
        for at in range(0, len(CHANS[group]), 2):
            cols = slice(at * 128, at * 128 + 256)
            field = product(left, (table[0, :, cols], table[1, :, cols]))
            use(CHANS[group][at], field[:, :128])
            use(CHANS[group][at + 1], field[:, 128:])

    def pointwise(source, weight, start):
        def block(at, carry):
            rows = pl.ds(pl.multiple_of(lax.rem(at, 4) * 32, 32), 32)
            first = lax.div(at, 4) * 4
            totals = [jnp.full((32, 128), start(first + i), F32) for i in range(4)]
            for b in range(channels):
                value = source[b, rows]
                for i in range(4):
                    totals[i] = totals[i] + weight(first + i, b) * value
            for i in range(4):
                point[first + i, rows] = totals[i]
            return carry

        lax.fori_loop(0, 20, block, 0)

    barrier = pltpu.get_barrier_semaphore()

    def greet(peer):
        pl.semaphore_signal(barrier, inc=1, device_id={"yslab": peer},
                            device_id_type=pl.DeviceIdType.MESH)

    each_peer(greet)
    pl.semaphore_wait(barrier, SLABS - 1)

    for group in range(3):
        forward_group(0, group, lambda c: sig[c], True)
    sf[...] = sig[...].astype(F32)
    pointwise(sf, lambda a, b: mix[b, a], lambda a: bias[a])
    for group in range(3):
        wait_chunk(0, group)
        spectra(0, group, modes, scale_fwd)

    for jl in range(2):
        rows = slice(jl * 16, jl * 16 + 16)

        def add(c, total):
            real, imag = total
            wr = w[rows, pl.ds(pl.multiple_of(c * 640, 128), 640)].astype(F32)
            wi = w[rows, pl.ds(pl.multiple_of(c * 640 + 12800, 128), 640)].astype(F32)
            value = modes[jl, c]
            ur = jnp.concatenate([value[:, :128]] * 5, axis=1)
            ui = jnp.concatenate([value[:, 128:]] * 5, axis=1)
            return real + wr * ur - wi * ui, imag + wr * ui + wi * ur

        zero = jnp.zeros((16, 640), F32)
        real, imag = lax.fori_loop(0, channels, add, (zero, zero))
        for oq in range(5):
            cols = slice(oq * 128, (oq + 1) * 128)
            if oq < 4:
                starts = [jl * 64 + oq * 16]
            else:
                starts = [128 + dup * 32 + jl * 16 for dup in range(4)]
            for row in starts:
                spec[row:row + 16, :128] = real[:, cols]
                spec[row:row + 16, 128:] = imag[:, cols]
    grid = product(both(tyi), halves(spec[...] * scale_inv), ((1,), (1,)))
    last = jnp.zeros((128, 128), F32)
    for i in range(4):
        send[1, :, i] = grid[i * 128:(i + 1) * 128, :128].reshape(16, 8, 128)
        last = jnp.where(lane // 32 == i, grid[i * 128:(i + 1) * 128, 128:], last)
    send[1, :, 4] = last.reshape(16, 8, 128)
    for group in range(3):
        send_chunk(1, group)

    def activate(o, field):
        value = field + point[o]
        root = math.sqrt(2.0 / math.pi)
        square = value * value
        t = jnp.tanh(root * value * (1.0 + 0.044715 * square))
        half = 0.5 * (1.0 + t)
        act[o] = (value * half).astype(BF16)
        slope = half + 0.5 * value * (1.0 - t * t) * root * (1.0 + 3 * 0.044715 * square)
        dpre[o] = cot[o].astype(F32) * slope

    for group in range(3):
        wait_chunk(1, group)
        back_group(1, group, activate)
        forward_group(2, group, lambda c: dpre[c], False)

    pointwise(dpre, lambda a, b: mix[a, b], lambda a: 0.0)

    def reduce_rows(value):
        return jnp.sum(value, axis=0, keepdims=True)

    def pair_sums(c, carry):
        field = sf[c]
        for o in range(channels):
            gmix[c, o:o + 1] = reduce_rows(field * dpre[o])
        return carry

    gmix[...] = jnp.zeros_like(gmix)
    lax.fori_loop(0, channels, pair_sums, 0)
    for o in range(channels):
        gmix[channels, o:o + 1] = reduce_rows(dpre[o])
    flat = jnp.concatenate([gmix[...].reshape(504, 128), jnp.zeros((8, 128), F32)], axis=0)
    line = lax.broadcasted_iota(jnp.int32, (8, 128), 0)
    ones = jnp.ones((8, 128), BF16)
    packed = jnp.zeros((8, 128), F32)
    for r in range(4):
        high, low = halves(flat[r * 128:(r + 1) * 128])
        value = product((ones, None), (high, low), ((1,), (1,)))
        packed = jnp.where(line == r, value, packed)
    sums[pl.ds(me, 1)] = (packed * scale_fwd).reshape(1, 8, 128)
    each_peer(lambda peer: sum_copy(peer, me).start())

    for group in range(3):
        wait_chunk(2, group)
        spectra(2, group, dmodes, scale_inv)

    lanes = lax.broadcasted_iota(jnp.int32, (16, 128), 1) // 32
    for jl in range(2):
        rows = slice(jl * 16, jl * 16 + 16)
        parts = []
        for ri in range(2):
            tiles = []
            for oq in range(5):
                tile = dmodes[jl, oq * 4, :, ri * 128:ri * 128 + 128]
                for i in range(1, 4):
                    other = dmodes[jl, oq * 4 + i, :, ri * 128:ri * 128 + 128]
                    tile = jnp.where(lanes == i, other, tile)
                tiles.append(tile)
            parts.append(jnp.concatenate(tiles, axis=1))
        dr, di = parts

        for c in range(channels):
            wr = w[rows, c * 640:c * 640 + 640].astype(F32)
            wi = w[rows, c * 640 + 12800:c * 640 + 13440].astype(F32)
            real = wr * dr + wi * di
            imag = wr * di - wi * dr
            if c < 16:
                row = (c % 4) * 128 + jl * 64 + (c // 4) * 16
            else:
                row = 512 + (c - 16) * 32 + jl * 16
            for ri, value in ((0, real), (1, imag)):
                folded = value[:, :128]
                for oq in range(1, 5):
                    folded = folded + value[:, oq * 128:(oq + 1) * 128]
                dspec[row:row + 16, ri * 128:ri * 128 + 128] = folded
    for t in range(5):
        grid = product(both(tyr), halves(dspec[t * 128:(t + 1) * 128] * scale_fwd), ((1,), (1,)))
        send[3, :, t] = grid.reshape(16, 8, 128)
        if t == 1 or t == 3 or t == 4:
            send_chunk(3, t // 2)

    for jl in range(2):
        rows = slice(jl * 16, jl * 16 + 16)
        parts = []
        for ri in range(2):
            tiles = []
            for oq in range(5):
                tile = dmodes[jl, oq * 4, :, ri * 128:ri * 128 + 128]
                for i in range(1, 4):
                    other = dmodes[jl, oq * 4 + i, :, ri * 128:ri * 128 + 128]
                    tile = jnp.where(lanes == i, other, tile)
                tiles.append(tile)
            parts.append(jnp.concatenate(tiles, axis=1))
        dr, di = parts

        def outer(c, carry):
            value = modes[jl, c]
            ur = jnp.concatenate([value[:, :128]] * 5, axis=1)
            ui = jnp.concatenate([value[:, 128:]] * 5, axis=1)
            gspec[rows, pl.ds(pl.multiple_of(c * 640, 128), 640)] = ur * dr + ui * di
            gspec[rows, pl.ds(pl.multiple_of(c * 640 + 12800, 128), 640)] = ur * di - ui * dr
            return carry

        lax.fori_loop(0, channels, outer, 0)

    each_peer(lambda peer: sum_copy(peer, peer).wait_recv())
    gsum[...] = jnp.sum(sums[...], axis=0)

    def finish(c, field):
        gin[c] = (field + point[c]).astype(BF16)

    for group in range(3):
        wait_chunk(3, group)
        back_group(3, group, finish)

    each_peer(lambda peer: sum_copy(peer, me).wait_send())
    for step in range(4):
        for group in range(3):
            each_peer(lambda peer: copy(step, group, peer).wait_send())


def per_device(signal, cotangent, spectral_weight, mix_weight, mix_bias):
    channels, width_x, rows_y, width_z = signal.shape
    slabs = lax.axis_size("yslab")
    if (channels, width_x, rows_y, width_z, slabs) != (20, 32, ROWS, 128, SLABS):
        return per_device_general(signal, cotangent, spectral_weight, mix_weight, mix_bias)
    length_y = rows_y * slabs
    scale_fwd = 1.0 / math.sqrt(width_x * length_y * width_z)
    scale_inv = 1.0 / math.sqrt(4 * MODES**3)
    tables_in = [jnp.asarray(t) for t in host_tables(width_x, length_y, width_z)]
    flat = (channels, width_x * rows_y, width_z)
    vmem = pl.BlockSpec(memory_space=pltpu.VMEM)
    smem = pl.BlockSpec(memory_space=pltpu.SMEM)
    act, gin, gspec, gsum = pl.pallas_call(
        partial(block_kernel, scale_fwd, scale_inv),
        out_shape=(
            jax.ShapeDtypeStruct(flat, BF16),
            jax.ShapeDtypeStruct(flat, BF16),
            jax.ShapeDtypeStruct(spectral_weight.shape, F32),
            jax.ShapeDtypeStruct((8, 128), F32),
        ),
        in_specs=[vmem, vmem, vmem, smem, smem] + [vmem] * len(tables_in),
        out_specs=(vmem, vmem, vmem, vmem),
        scratch_shapes=[
            pltpu.VMEM(flat, F32),
            pltpu.VMEM(flat, F32),
            pltpu.VMEM(flat, F32),
            pltpu.VMEM((2, 20, 16, 256), F32),
            pltpu.VMEM((2, 20, 16, 256), F32),
            pltpu.VMEM((256, 256), F32),
            pltpu.VMEM((640, 256), F32),
            pltpu.VMEM((21, 24, 128), F32),
            pltpu.VMEM((4, SLABS, 5, 8, 128), F32),
            pltpu.VMEM((4, SLABS, 5, 8, 128), F32),
            pltpu.VMEM((SLABS, 8, 128), F32),
            pltpu.SemaphoreType.DMA((4, 3, SLABS)),
            pltpu.SemaphoreType.DMA((4, 3, SLABS)),
            pltpu.SemaphoreType.DMA((SLABS,)),
            pltpu.SemaphoreType.DMA((SLABS,)),
        ],
        compiler_params=pltpu.CompilerParams(
            collective_id=0, has_side_effects=True, vmem_limit_bytes=48 * 1024 * 1024
        ),
    )(
        signal.reshape(flat), cotangent.reshape(flat), spectral_weight, mix_weight, mix_bias,
        *tables_in,
    )
    full = gsum[:4].reshape(512)[:504].reshape(21, 24)
    return (
        act.reshape(signal.shape), gin.reshape(signal.shape), gspec, full[:20, :20], full[20, :20],
    )


def solution(mesh):
    placed = (
        P(None, "groups", "yslab", None),
        P(None, "groups", "yslab", None),
        P("yslab", None),
        P(),
        P(),
    )
    return jax.shard_map(
        per_device,
        mesh=mesh,
        in_specs=placed,
        out_specs=(
            P(None, "groups", "yslab", None),
            P(None, "groups", "yslab", None),
            P("yslab", "groups"),
            P("groups", None),
            P("groups"),
        ),
        check_vma=False,
    )
```

```python
from functools import partial
import math

import ml_dtypes
import numpy as np

import jax
import jax.numpy as jnp
from jax import lax
from jax.experimental import pallas as pl
from jax.experimental.pallas import tpu as pltpu
from jax.sharding import PartitionSpec as P

MODES = 16
PAIRS = 512


def contract(form, left, right):
    return jnp.einsum(
        form, left, right, precision=lax.Precision.HIGH, preferred_element_type=jnp.float32
    )


def signed_waves(modes):
    return jnp.concatenate(
        [jnp.arange(modes, dtype=jnp.int32), jnp.arange(-modes, 0, dtype=jnp.int32)]
    )


def tables(places, length, wavenum):
    phase = jnp.mod(places[:, None] * wavenum[None, :], length).astype(jnp.float32)
    angle = phase * (2.0 * math.pi / length)
    return (jnp.cos(angle), jnp.sin(angle))


def per_device_general(signal, cotangent, spectral_weight, mix_weight, mix_bias):
    channels, width_x, rows_y, width_z = signal.shape
    slabs = lax.axis_size("yslab")
    length_y = rows_y * slabs
    waves = signed_waves(MODES)
    cos_x, sin_x = tables(jnp.arange(width_x, dtype=jnp.int32), width_x, waves)
    cos_z, sin_z = tables(
        jnp.arange(width_z, dtype=jnp.int32), width_z, jnp.arange(MODES, dtype=jnp.int32)
    )
    scale_fwd = 1.0 / math.sqrt(width_x * length_y * width_z)
    scale_inv = 1.0 / math.sqrt(4 * MODES**3)

    all_rows = jnp.arange(length_y, dtype=jnp.int32)
    cos_y, sin_y = tables(all_rows, length_y, waves)
    turn_y = jnp.stack(
        [jnp.stack([cos_y, -sin_y], axis=1), jnp.stack([sin_y, cos_y], axis=1)]
    ).reshape(2, slabs, rows_y, 2, 2 * MODES)
    owned = PAIRS // slabs
    back_x = jnp.stack([jnp.stack([cos_x, sin_x]), jnp.stack([-sin_x, cos_x])])
    turn_z = jnp.stack([cos_z, -sin_z])

    def to_modes(field, scale):
        first = contract("cxyz,rzk->rcxyk", field, turn_z)
        second = contract(
            "rcxyk,rqxj->qcyjk", first, jnp.stack(
                [jnp.stack([cos_x, -sin_x]), jnp.stack([sin_x, cos_x])]
            )
        )
        blocks = second.reshape(2, channels, rows_y, slabs, owned)
        blocks = jnp.transpose(blocks, (3, 0, 2, 1, 4))
        rows = lax.all_to_all(blocks, "yslab", split_axis=0, concat_axis=0, tiled=True)
        return contract("sqycp,qsyrm->prcm", rows, turn_y) * scale

    def to_grid(spectrum, scale):
        rows = contract("prcm,rsyqm->sqycp", spectrum, jnp.transpose(turn_y, (3, 1, 2, 0, 4)))
        rows = lax.all_to_all(rows, "yslab", split_axis=0, concat_axis=0, tiled=True)
        shaped = jnp.transpose(rows, (1, 3, 2, 0, 4)).reshape(
            2, channels, rows_y, 2 * MODES, MODES
        )
        second = contract("qcyjk,qrxj->rcxyk", shaped, back_x)
        return contract("rcxyk,rzk->cxyz", second, turn_z) * scale

    weights = spectral_weight.astype(jnp.float32).reshape(-1, 2, channels, channels, 2 * MODES)
    w_real = weights[:, 0]
    w_imag = weights[:, 1]
    spectrum = to_modes(signal, scale_fwd)
    modes_re = spectrum[:, 0]
    modes_im = spectrum[:, 1]
    mixed_re = contract("pcom,pcm->pom", w_real, modes_re) - contract(
        "pcom,pcm->pom", w_imag, modes_im
    )
    mixed_im = contract("pcom,pcm->pom", w_real, modes_im) + contract(
        "pcom,pcm->pom", w_imag, modes_re
    )
    spectral = to_grid(jnp.stack([mixed_re, mixed_im], axis=1), scale_inv)
    pre = spectral + contract("cxyz,co->oxyz", signal, mix_weight) + mix_bias[:, None, None, None]
    result, pullback = jax.vjp(partial(jax.nn.gelu, approximate=True), pre)
    activation = result.astype(jnp.bfloat16)
    dpre = pullback(cotangent.astype(jnp.float32))[0]
    dmixed = to_modes(dpre, scale_inv)
    dmixed_re = dmixed[:, 0]
    dmixed_im = dmixed[:, 1]
    dweight_re = contract("pcm,pom->pcom", modes_re, dmixed_re) + contract(
        "pcm,pom->pcom", modes_im, dmixed_im
    )
    dweight_im = contract("pcm,pom->pcom", modes_re, dmixed_im) - contract(
        "pcm,pom->pcom", modes_im, dmixed_re
    )
    grad_spectral = jnp.stack([dweight_re, dweight_im], axis=1).reshape(
        spectral_weight.shape[0], -1
    )
    dmodes_re = contract("pcom,pom->pcm", w_real, dmixed_re) + contract(
        "pcom,pom->pcm", w_imag, dmixed_im
    )
    dmodes_im = contract("pcom,pom->pcm", w_real, dmixed_im) - contract(
        "pcom,pom->pcm", w_imag, dmixed_re
    )
    back_field = to_grid(jnp.stack([dmodes_re, dmodes_im], axis=1), scale_fwd)
    grad_input = (back_field + contract("oxyz,co->cxyz", dpre, mix_weight)).astype(jnp.bfloat16)
    mix_sum, bias_sum = lax.psum(
        (contract("cxyz,oxyz->co", signal, dpre), jnp.sum(dpre, axis=(1, 2, 3))), "yslab"
    )
    return (activation, grad_input, grad_spectral, mix_sum * scale_fwd, bias_sum * scale_fwd)


SLABS = 16
TABLES = {}
for name, rows in (("z8", 1024), ("wx", 256), ("z4", 512), ("ty", 128), ("tyi", 512),
                   ("wxi", 256), ("zi8", 1024), ("zi4", 512), ("tyr", 128)):
    TABLES[name] = (sum(count for _, count in TABLES.values()), rows)
ROWS = 4
F32 = jnp.float32
BF16 = jnp.bfloat16
CHANS = [[oq * 4 + 2 * q + ii for ii in range(2) for oq in range(4)] for q in range(2)]
CHANS.append([16, 17, 18, 19])
CHUNKS = [(0, 2), (2, 2), (4, 1)]


def split_table(table):
    high = table.astype(ml_dtypes.bfloat16)
    low = (table - high.astype(np.float64)).astype(ml_dtypes.bfloat16)
    return np.stack([high, low])


def host_waves(places, length, wavenum):
    angle = np.mod(np.outer(places, wavenum), length) * (2.0 * math.pi / length)
    return np.cos(angle), np.sin(angle)


def host_tables(width_x, length_y, width_z):
    waves = np.concatenate([np.arange(MODES), np.arange(-MODES, 0)])
    cx, sx = host_waves(np.arange(width_x), width_x, waves)
    cy, sy = host_waves(np.arange(length_y), length_y, waves)
    cz, sz = host_waves(np.arange(width_z), width_z, np.arange(MODES))
    eye_y = np.eye(ROWS)
    fz = np.stack([cz, -sz])
    z8 = np.einsum("ab,rzk->azrbk", np.eye(8), fz).reshape(8 * width_z, 256)
    z4 = np.einsum("ab,rzk,e->azrebk", np.eye(4), fz, np.ones(2)).reshape(4 * width_z, 256)
    fx = np.stack([np.stack([cx, -sx]), np.stack([sx, cx])])
    wx = np.einsum("rqxdl,yt->ldyqrxt", fx.reshape(2, 2, width_x, SLABS, 2), eye_y)
    wx = wx.reshape(256, 256)
    bx = np.stack([np.stack([cx, sx]), np.stack([-sx, cx])])
    wxi = np.einsum("qrxdl,yt->rxtldyq", bx.reshape(2, 2, width_x, SLABS, 2), eye_y)
    wxi = wxi.reshape(256, 256)
    fy = np.stack([np.stack([cy, -sy]), np.stack([sy, cy])])
    ty = np.einsum("rqym,e->yrqem", fy, np.ones(4)).reshape(128, 256)
    by = np.stack([np.stack([cy, sy]), np.stack([-sy, cy])])
    tyi = np.einsum("rqym,ie->iyqrem", by, np.eye(4)).reshape(512, 256)
    tyr = np.einsum("rqym,e->yqrem", by, np.ones(4)).reshape(128, 256)
    zi8 = np.einsum("ab,rzk->rakbz", np.eye(8), fz).reshape(256, 8 * width_z)
    pick = np.stack([np.ones(1), np.zeros(1)]).reshape(2)
    zi4 = np.einsum("ab,rzk,e->raekbz", np.eye(4), fz, pick).reshape(256, 4 * width_z)
    zi8 = np.concatenate(np.split(zi8, 4, axis=1))
    zi4 = np.concatenate(np.split(zi4, 2, axis=1))
    return split_table(np.concatenate([z8, wx, z4, ty, tyi, wxi, zi8, zi4, tyr]))


def halves(value):
    high = value.astype(BF16)
    return high, (value - high.astype(F32)).astype(BF16)


def product(left, right, form=((1,), (0,))):
    def one(a, b):
        return lax.dot_general(a, b, (form, ((), ())), preferred_element_type=F32)

    total = one(left[0], right[0])
    if left[1] is not None:
        total = total + one(left[1], right[0])
    if right[1] is not None:
        total = total + one(left[0], right[1])
    return total


def block_kernel(scale_fwd, scale_inv, *refs):
    sources, refs = refs[:4], refs[4:]
    mix, bias, act, gin, gspec, gsum, sf, point, dpre, modes, dmodes, spec, dspec, gmix = refs[:14]
    send, recv, sums, send_sem, recv_sem, sum_send, sum_recv, load_sem = refs[14:22]
    places = refs[22:]
    sig, tables, w, cot = places

    def table(name, first=0, count=None):
        start, rows = TABLES[name]
        rows = slice(start + first, start + first + (count or rows))
        return tables[0, rows], tables[1, rows]
    me = lax.axis_index("yslab")
    channels = 20
    lane = lax.broadcasted_iota(jnp.int32, (128, 128), 1)

    def copy(step, chunk, peer):
        first, count = CHUNKS[chunk]
        return pltpu.make_async_remote_copy(
            src_ref=send.at[step, peer, pl.ds(first, count)],
            dst_ref=recv.at[step, me, pl.ds(first, count)],
            send_sem=send_sem.at[step, chunk, peer],
            recv_sem=recv_sem.at[step, chunk, me],
            device_id={"yslab": peer},
            device_id_type=pl.DeviceIdType.MESH,
        )

    def arrival(step, chunk, peer):
        first, count = CHUNKS[chunk]
        return pltpu.make_async_remote_copy(
            src_ref=send.at[step, peer, pl.ds(first, count)],
            dst_ref=recv.at[step, peer, pl.ds(first, count)],
            send_sem=send_sem.at[step, chunk, peer],
            recv_sem=recv_sem.at[step, chunk, peer],
            device_id={"yslab": peer},
            device_id_type=pl.DeviceIdType.MESH,
        )

    def sum_copy(peer, source):
        return pltpu.make_async_remote_copy(
            src_ref=sums.at[me],
            dst_ref=sums.at[source],
            send_sem=sum_send.at[peer],
            recv_sem=sum_recv.at[source],
            device_id={"yslab": peer},
            device_id_type=pl.DeviceIdType.MESH,
        )

    def each_peer(action):
        def body(i, carry):
            shift = 8 + lax.div(i, 2) * (1 - 2 * lax.rem(i, 2))
            action(lax.rem(me + shift, SLABS))
            return carry

        lax.fori_loop(1, SLABS, body, 0)

    def send_chunk(step, chunk):
        each_peer(lambda peer: copy(step, chunk, peer).start())
        first, count = CHUNKS[chunk]
        recv[step, pl.ds(me, 1), first:first + count] = send[step, pl.ds(me, 1), first:first + count]

    def wait_chunk(step, chunk):
        each_peer(lambda peer: arrival(step, chunk, peer).wait_recv())

    def forward_group(step, group, read, exact):
        name = "z8" if group < 2 else "z4"
        total = None
        for at in range(0, len(CHANS[group]), 2):
            pair = jnp.concatenate([read(c) for c in CHANS[group][at:at + 2]], axis=1)
            left = (pair, None) if exact else halves(pair)
            part = product(left, table(name, at * 128, 256))
            total = part if total is None else total + part
        stacked = jnp.concatenate([total[:, :128], total[:, 128:]], axis=0)
        out = product(table("wx"), halves(stacked))
        if group < 2:
            for jl in range(2):
                send[step, :, 2 * group + jl] = out[jl * 128:(jl + 1) * 128].reshape(16, 8, 128)
        else:
            send[step, :, 4] = jnp.where(lane < 64, out[:128], out[128:]).reshape(16, 8, 128)
        send_chunk(step, group)

    def spectra(step, group, target, scale):
        for jl in range(2 if group < 2 else 1):
            tile = recv[step, :, 2 * group + jl].reshape(128, 128) * scale
            out = product(halves(tile.T), table("ty"))
            if group < 2:
                for place, c in enumerate(CHANS[group]):
                    target[jl, c] = out[place * 16:(place + 1) * 16]
            else:
                for jj in range(2):
                    for place, c in enumerate(CHANS[2]):
                        row = jj * 64 + place * 16
                        target[jj, c] = out[row:row + 16]

    def back_group(step, group, use):
        if group < 2:
            one = recv[step, :, 2 * group].reshape(128, 128)
            two = recv[step, :, 2 * group + 1].reshape(128, 128)
            top = jnp.where(lane < 64, one, pltpu.roll(two, 64, 1))
            low = jnp.where(lane < 64, pltpu.roll(one, 64, 1), two)
        else:
            top = recv[step, :, 4].reshape(128, 128)
            low = pltpu.roll(top, 112, 1)
        out = product(table("wxi"), halves(jnp.concatenate([top, low], axis=0)))
        left = halves(jnp.concatenate([out[:128], out[128:]], axis=1))
        name = "zi8" if group < 2 else "zi4"
        for at in range(0, len(CHANS[group]), 2):
            field = product(left, table(name, at * 128, 256))
            use(CHANS[group][at], field[:, :128])
            use(CHANS[group][at + 1], field[:, 128:])

    def pointwise(source, weight, start):
        def block(at, carry):
            rows = pl.ds(pl.multiple_of(lax.rem(at, 4) * 32, 32), 32)
            first = lax.div(at, 4) * 4
            totals = [jnp.full((32, 128), start(first + i), F32) for i in range(4)]
            for b in range(channels):
                value = source[b, rows]
                for i in range(4):
                    totals[i] = totals[i] + weight(first + i, b) * value
            for i in range(4):
                point[first + i, rows] = totals[i]
            return carry

        lax.fori_loop(0, 20, block, 0)

    def rows_of(first, last):
        return pl.ds(TABLES[first][0], TABLES[last][0] + TABLES[last][1] - TABLES[first][0])

    early, late = rows_of("z8", "z4"), rows_of("ty", "tyr")

    def load(index):
        source, place = sources[index % 4], places[index % 4]
        if index in (1, 5):
            rows = early if index == 1 else late
            source, place = source.at[:, rows], place.at[:, rows]
        return pltpu.make_async_copy(source, place, load_sem.at[index])

    def loaded(*indices):
        for index in indices:
            load(index).wait()

    for index in (0, 1, 2, 5, 3):
        load(index).start()

    barrier = pltpu.get_barrier_semaphore()

    def greet(peer):
        pl.semaphore_signal(barrier, inc=1, device_id={"yslab": peer},
                            device_id_type=pl.DeviceIdType.MESH)

    each_peer(greet)
    pl.semaphore_wait(barrier, SLABS - 1)

    loaded(0, 1)

    for group in range(3):
        forward_group(0, group, lambda c: sig[c], True)
    sf[...] = sig[...].astype(F32)
    pointwise(sf, lambda a, b: mix[b, a], lambda a: bias[a])
    loaded(2, 5, 3)

    mixed = [(jnp.zeros((16, 640), F32), jnp.zeros((16, 640), F32)) for jl in range(2)]
    for group in range(3):
        wait_chunk(0, group)
        spectra(0, group, modes, scale_fwd)
        for jl in range(2):
            rows = slice(jl * 16, jl * 16 + 16)

            def add(n, total):
                if group < 2:
                    c = lax.rem(n, 4) * 4 + 2 * group + lax.div(n, 4)
                else:
                    c = 16 + n
                real, imag = total
                wr = w[rows, pl.ds(pl.multiple_of(c * 640, 128), 640)].astype(F32)
                wi = w[rows, pl.ds(pl.multiple_of(c * 640 + 12800, 128), 640)].astype(F32)
                value = modes[jl, c]
                ur = jnp.concatenate([value[:, :128]] * 5, axis=1)
                ui = jnp.concatenate([value[:, 128:]] * 5, axis=1)
                return real + wr * ur - wi * ui, imag + wr * ui + wi * ur

            mixed[jl] = lax.fori_loop(0, len(CHANS[group]), add, mixed[jl])
    for jl in range(2):
        real, imag = mixed[jl]
        for oq in range(5):
            cols = slice(oq * 128, (oq + 1) * 128)
            if oq < 4:
                starts = [jl * 64 + oq * 16]
            else:
                starts = [128 + dup * 32 + jl * 16 for dup in range(4)]
            for row in starts:
                spec[row:row + 16, :128] = real[:, cols]
                spec[row:row + 16, 128:] = imag[:, cols]
    last = jnp.zeros((128, 128), F32)
    right = halves(spec[...] * scale_inv)
    for q in range(2):
        grid = product(table("tyi", q * 256, 256), right, ((1,), (1,)))
        for ii in range(2):
            part = grid[ii * 128:(ii + 1) * 128]
            send[1, :, 2 * q + ii] = part[:, :128].reshape(16, 8, 128)
            last = jnp.where(lane // 32 == 2 * q + ii, part[:, 128:], last)
        send_chunk(1, q)
    send[1, :, 4] = last.reshape(16, 8, 128)
    send_chunk(1, 2)

    def activate(o, field):
        value = field + point[o]
        root = math.sqrt(2.0 / math.pi)
        square = value * value
        t = jnp.tanh(root * value * (1.0 + 0.044715 * square))
        half = 0.5 * (1.0 + t)
        act[o] = (value * half).astype(BF16)
        slope = half + 0.5 * value * (1.0 - t * t) * root * (1.0 + 3 * 0.044715 * square)
        dpre[o] = cot[o].astype(F32) * slope

    for group in range(3):
        wait_chunk(1, group)
        back_group(1, group, activate)
        forward_group(2, group, lambda c: dpre[c], False)


    def reduce_rows(value):
        return jnp.sum(value, axis=0, keepdims=True)

    def pair_sums(c, carry):
        field = sf[c]
        for o in range(channels):
            gmix[c, o:o + 1] = reduce_rows(field * dpre[o])
        return carry

    gmix[...] = jnp.zeros_like(gmix)
    lax.fori_loop(0, channels, pair_sums, 0)
    for o in range(channels):
        gmix[channels, o:o + 1] = reduce_rows(dpre[o])
    flat = gmix[...].reshape(768, 128)
    line = lax.broadcasted_iota(jnp.int32, (8, 128), 0)
    ones = jnp.ones((8, 128), BF16)
    packed = jnp.zeros((8, 128), F32)
    for r in range(6):
        high, low = halves(flat[r * 128:(r + 1) * 128])
        value = product((ones, None), (high, low), ((1,), (1,)))
        packed = jnp.where(line == r, value, packed)
    sums[pl.ds(me, 1)] = (packed * scale_fwd).reshape(1, 8, 128)
    each_peer(lambda peer: sum_copy(peer, me).start())

    for group in range(3):
        wait_chunk(2, group)
        spectra(2, group, dmodes, scale_inv)

    lanes = lax.broadcasted_iota(jnp.int32, (16, 128), 1) // 32
    for jl in range(2):
        rows = slice(jl * 16, jl * 16 + 16)
        parts = []
        for ri in range(2):
            tiles = []
            for oq in range(5):
                tile = dmodes[jl, oq * 4, :, ri * 128:ri * 128 + 128]
                for i in range(1, 4):
                    other = dmodes[jl, oq * 4 + i, :, ri * 128:ri * 128 + 128]
                    tile = jnp.where(lanes == i, other, tile)
                tiles.append(tile)
            parts.append(jnp.concatenate(tiles, axis=1))
        dr, di = parts

        for c in range(channels):
            wr = w[rows, c * 640:c * 640 + 640].astype(F32)
            wi = w[rows, c * 640 + 12800:c * 640 + 13440].astype(F32)
            real = wr * dr + wi * di
            imag = wr * di - wi * dr
            if c < 16:
                row = (c % 4) * 128 + jl * 64 + (c // 4) * 16
            else:
                row = 512 + (c - 16) * 32 + jl * 16
            for ri, value in ((0, real), (1, imag)):
                folded = value[:, :128]
                for oq in range(1, 5):
                    folded = folded + value[:, oq * 128:(oq + 1) * 128]
                dspec[row:row + 16, ri * 128:ri * 128 + 128] = folded
    for t in range(5):
        grid = product(table("tyr"), halves(dspec[t * 128:(t + 1) * 128] * scale_fwd), ((1,), (1,)))
        send[3, :, t] = grid.reshape(16, 8, 128)
        if t == 1 or t == 3 or t == 4:
            send_chunk(3, t // 2)

    for jl in range(2):
        rows = slice(jl * 16, jl * 16 + 16)
        parts = []
        for ri in range(2):
            tiles = []
            for oq in range(5):
                tile = dmodes[jl, oq * 4, :, ri * 128:ri * 128 + 128]
                for i in range(1, 4):
                    other = dmodes[jl, oq * 4 + i, :, ri * 128:ri * 128 + 128]
                    tile = jnp.where(lanes == i, other, tile)
                tiles.append(tile)
            parts.append(jnp.concatenate(tiles, axis=1))
        dr, di = parts

        def outer(c, carry):
            value = modes[jl, c]
            ur = jnp.concatenate([value[:, :128]] * 5, axis=1)
            ui = jnp.concatenate([value[:, 128:]] * 5, axis=1)
            gspec[rows, pl.ds(pl.multiple_of(c * 640, 128), 640)] = ur * dr + ui * di
            gspec[rows, pl.ds(pl.multiple_of(c * 640 + 12800, 128), 640)] = ur * di - ui * dr
            return carry

        lax.fori_loop(0, channels, outer, 0)

    pointwise(dpre, lambda a, b: mix[a, b], lambda a: 0.0)
    each_peer(lambda peer: sum_copy(peer, peer).wait_recv())
    gsum[...] = jnp.sum(sums[...], axis=0)

    def finish(c, field):
        gin[c] = (field + point[c]).astype(BF16)

    for group in range(3):
        wait_chunk(3, group)
        back_group(3, group, finish)

    each_peer(lambda peer: sum_copy(peer, me).wait_send())
    for step in range(4):
        for group in range(3):
            each_peer(lambda peer: copy(step, group, peer).wait_send())


def write_kernel(*refs):
    sums, sources = refs[0], refs[1:4]
    outs, gmix, gbias, sems = refs[4:7], refs[7], refs[8], refs[9]
    copies = [pltpu.make_async_copy(sources[i], outs[i], sems.at[i]) for i in range(3)]
    for copy in copies:
        copy.start()
    packed = sums[...]
    for c in range(20):
        at = (c % 4) * 32
        gmix[c:c + 1, :] = packed[c // 4:c // 4 + 1, at:at + 20]
    gbias[...] = packed[5:6, :20]
    for copy in copies:
        copy.wait()


def per_device(signal, cotangent, spectral_weight, mix_weight, mix_bias):
    channels, width_x, rows_y, width_z = signal.shape
    slabs = lax.axis_size("yslab")
    if (channels, width_x, rows_y, width_z, slabs) != (20, 32, ROWS, 128, SLABS):
        return per_device_general(signal, cotangent, spectral_weight, mix_weight, mix_bias)
    length_y = rows_y * slabs
    scale_fwd = 1.0 / math.sqrt(width_x * length_y * width_z)
    scale_inv = 1.0 / math.sqrt(4 * MODES**3)
    flat = (channels, width_x * rows_y, width_z)
    packed = jnp.asarray(host_tables(width_x, length_y, width_z))
    sources = [signal.reshape(flat), packed, spectral_weight, cotangent.reshape(flat)]
    vmem = pl.BlockSpec(memory_space=pltpu.VMEM)
    smem = pl.BlockSpec(memory_space=pltpu.SMEM)
    hbm = pl.BlockSpec(memory_space=pltpu.HBM)
    wide = jax.ShapeDtypeStruct(spectral_weight.shape, F32)
    grid = jax.ShapeDtypeStruct(flat, BF16)
    act, gin, gspec, gsum = pl.pallas_call(
        partial(block_kernel, scale_fwd, scale_inv),
        out_shape=(grid, grid, wide, jax.ShapeDtypeStruct((8, 128), F32)),
        in_specs=[hbm] * 4 + [smem, smem],
        out_specs=(vmem, vmem, vmem, vmem),
        scratch_shapes=[
            pltpu.VMEM(flat, F32),
            pltpu.VMEM(flat, F32),
            pltpu.VMEM(flat, F32),
            pltpu.VMEM((2, 20, 16, 256), F32),
            pltpu.VMEM((2, 20, 16, 256), F32),
            pltpu.VMEM((256, 256), F32),
            pltpu.VMEM((640, 256), F32),
            pltpu.VMEM((24, 32, 128), F32),
            pltpu.VMEM((4, SLABS, 5, 8, 128), F32),
            pltpu.VMEM((4, SLABS, 5, 8, 128), F32),
            pltpu.VMEM((SLABS, 8, 128), F32),
            pltpu.SemaphoreType.DMA((4, 3, SLABS)),
            pltpu.SemaphoreType.DMA((4, 3, SLABS)),
            pltpu.SemaphoreType.DMA((SLABS,)),
            pltpu.SemaphoreType.DMA((SLABS,)),
            pltpu.SemaphoreType.DMA((6,)),
        ] + [pltpu.VMEM(x.shape, x.dtype) for x in sources],
        compiler_params=pltpu.CompilerParams(
            collective_id=0, has_side_effects=True, vmem_limit_bytes=30 * 1024 * 1024
        ),
    )(*sources, mix_weight, mix_bias)
    act, gin, gspec, gmix, gbias = pl.pallas_call(
        write_kernel,
        out_shape=(
            grid, grid, wide,
            jax.ShapeDtypeStruct((20, 20), F32), jax.ShapeDtypeStruct((1, 20), F32),
        ),
        in_specs=[vmem] * 4,
        out_specs=(hbm, hbm, hbm, vmem, vmem),
        scratch_shapes=[pltpu.SemaphoreType.DMA((3,))],
    )(gsum, act, gin, gspec)
    return act.reshape(signal.shape), gin.reshape(signal.shape), gspec, gmix, gbias.reshape(20)


def solution(mesh):
    placed = (
        P(None, "groups", "yslab", None),
        P(None, "groups", "yslab", None),
        P("yslab", None),
        P(),
        P(),
    )
    return jax.shard_map(
        per_device,
        mesh=mesh,
        in_specs=placed,
        out_specs=(
            P(None, "groups", "yslab", None),
            P(None, "groups", "yslab", None),
            P("yslab", "groups"),
            P("groups", None),
            P("groups"),
        ),
        check_vma=False,
    )
```

```python
from functools import partial
import math

import ml_dtypes
import numpy as np

import jax
import jax.numpy as jnp
from jax import lax
from jax.experimental import pallas as pl
from jax.experimental.pallas import tpu as pltpu
from jax.sharding import PartitionSpec as P

MODES = 16
PAIRS = 512


def contract(form, left, right):
    return jnp.einsum(
        form, left, right, precision=lax.Precision.HIGH, preferred_element_type=jnp.float32
    )


def signed_waves(modes):
    return jnp.concatenate(
        [jnp.arange(modes, dtype=jnp.int32), jnp.arange(-modes, 0, dtype=jnp.int32)]
    )


def tables(places, length, wavenum):
    phase = jnp.mod(places[:, None] * wavenum[None, :], length).astype(jnp.float32)
    angle = phase * (2.0 * math.pi / length)
    return (jnp.cos(angle), jnp.sin(angle))


def per_device_general(signal, cotangent, spectral_weight, mix_weight, mix_bias):
    channels, width_x, rows_y, width_z = signal.shape
    slabs = lax.axis_size("yslab")
    length_y = rows_y * slabs
    waves = signed_waves(MODES)
    cos_x, sin_x = tables(jnp.arange(width_x, dtype=jnp.int32), width_x, waves)
    cos_z, sin_z = tables(
        jnp.arange(width_z, dtype=jnp.int32), width_z, jnp.arange(MODES, dtype=jnp.int32)
    )
    scale_fwd = 1.0 / math.sqrt(width_x * length_y * width_z)
    scale_inv = 1.0 / math.sqrt(4 * MODES**3)

    all_rows = jnp.arange(length_y, dtype=jnp.int32)
    cos_y, sin_y = tables(all_rows, length_y, waves)
    turn_y = jnp.stack(
        [jnp.stack([cos_y, -sin_y], axis=1), jnp.stack([sin_y, cos_y], axis=1)]
    ).reshape(2, slabs, rows_y, 2, 2 * MODES)
    owned = PAIRS // slabs
    back_x = jnp.stack([jnp.stack([cos_x, sin_x]), jnp.stack([-sin_x, cos_x])])
    turn_z = jnp.stack([cos_z, -sin_z])

    def to_modes(field, scale):
        first = contract("cxyz,rzk->rcxyk", field, turn_z)
        second = contract(
            "rcxyk,rqxj->qcyjk", first, jnp.stack(
                [jnp.stack([cos_x, -sin_x]), jnp.stack([sin_x, cos_x])]
            )
        )
        blocks = second.reshape(2, channels, rows_y, slabs, owned)
        blocks = jnp.transpose(blocks, (3, 0, 2, 1, 4))
        rows = lax.all_to_all(blocks, "yslab", split_axis=0, concat_axis=0, tiled=True)
        return contract("sqycp,qsyrm->prcm", rows, turn_y) * scale

    def to_grid(spectrum, scale):
        rows = contract("prcm,rsyqm->sqycp", spectrum, jnp.transpose(turn_y, (3, 1, 2, 0, 4)))
        rows = lax.all_to_all(rows, "yslab", split_axis=0, concat_axis=0, tiled=True)
        shaped = jnp.transpose(rows, (1, 3, 2, 0, 4)).reshape(
            2, channels, rows_y, 2 * MODES, MODES
        )
        second = contract("qcyjk,qrxj->rcxyk", shaped, back_x)
        return contract("rcxyk,rzk->cxyz", second, turn_z) * scale

    weights = spectral_weight.astype(jnp.float32).reshape(-1, 2, channels, channels, 2 * MODES)
    w_real = weights[:, 0]
    w_imag = weights[:, 1]
    spectrum = to_modes(signal, scale_fwd)
    modes_re = spectrum[:, 0]
    modes_im = spectrum[:, 1]
    mixed_re = contract("pcom,pcm->pom", w_real, modes_re) - contract(
        "pcom,pcm->pom", w_imag, modes_im
    )
    mixed_im = contract("pcom,pcm->pom", w_real, modes_im) + contract(
        "pcom,pcm->pom", w_imag, modes_re
    )
    spectral = to_grid(jnp.stack([mixed_re, mixed_im], axis=1), scale_inv)
    pre = spectral + contract("cxyz,co->oxyz", signal, mix_weight) + mix_bias[:, None, None, None]
    result, pullback = jax.vjp(partial(jax.nn.gelu, approximate=True), pre)
    activation = result.astype(jnp.bfloat16)
    dpre = pullback(cotangent.astype(jnp.float32))[0]
    dmixed = to_modes(dpre, scale_inv)
    dmixed_re = dmixed[:, 0]
    dmixed_im = dmixed[:, 1]
    dweight_re = contract("pcm,pom->pcom", modes_re, dmixed_re) + contract(
        "pcm,pom->pcom", modes_im, dmixed_im
    )
    dweight_im = contract("pcm,pom->pcom", modes_re, dmixed_im) - contract(
        "pcm,pom->pcom", modes_im, dmixed_re
    )
    grad_spectral = jnp.stack([dweight_re, dweight_im], axis=1).reshape(
        spectral_weight.shape[0], -1
    )
    dmodes_re = contract("pcom,pom->pcm", w_real, dmixed_re) + contract(
        "pcom,pom->pcm", w_imag, dmixed_im
    )
    dmodes_im = contract("pcom,pom->pcm", w_real, dmixed_im) - contract(
        "pcom,pom->pcm", w_imag, dmixed_re
    )
    back_field = to_grid(jnp.stack([dmodes_re, dmodes_im], axis=1), scale_fwd)
    grad_input = (back_field + contract("oxyz,co->cxyz", dpre, mix_weight)).astype(jnp.bfloat16)
    mix_sum, bias_sum = lax.psum(
        (contract("cxyz,oxyz->co", signal, dpre), jnp.sum(dpre, axis=(1, 2, 3))), "yslab"
    )
    return (activation, grad_input, grad_spectral, mix_sum * scale_fwd, bias_sum * scale_fwd)


SLABS = 16
TABLES = {}
for name, rows in (("z8", 1024), ("wx", 256), ("z4", 512), ("ty", 128), ("tyi", 512),
                   ("wxi", 256), ("zi8", 1024), ("zi4", 512), ("tyr", 128)):
    TABLES[name] = (sum(count for _, count in TABLES.values()), rows)
ROWS = 4
F32 = jnp.float32
BF16 = jnp.bfloat16
CHANS = [[oq * 4 + 2 * q + ii for ii in range(2) for oq in range(4)] for q in range(2)]
CHANS.append([16, 17, 18, 19])
CHUNKS = [(0, 2), (2, 2), (4, 1)]


def split_table(table):
    high = table.astype(ml_dtypes.bfloat16)
    low = (table - high.astype(np.float64)).astype(ml_dtypes.bfloat16)
    return np.stack([high, low])


def host_waves(places, length, wavenum):
    angle = np.mod(np.outer(places, wavenum), length) * (2.0 * math.pi / length)
    return np.cos(angle), np.sin(angle)


def host_tables(width_x, length_y, width_z):
    waves = np.concatenate([np.arange(MODES), np.arange(-MODES, 0)])
    cx, sx = host_waves(np.arange(width_x), width_x, waves)
    cy, sy = host_waves(np.arange(length_y), length_y, waves)
    cz, sz = host_waves(np.arange(width_z), width_z, np.arange(MODES))
    eye_y = np.eye(ROWS)
    fz = np.stack([cz, -sz])
    z8 = np.einsum("ab,rzk->azrbk", np.eye(8), fz).reshape(8 * width_z, 256)
    z4 = np.einsum("ab,rzk,e->azrebk", np.eye(4), fz, np.ones(2)).reshape(4 * width_z, 256)
    fx = np.stack([np.stack([cx, -sx]), np.stack([sx, cx])])
    wx = np.einsum("rqxdl,yt->ldyqrxt", fx.reshape(2, 2, width_x, SLABS, 2), eye_y)
    wx = wx.reshape(256, 256)
    bx = np.stack([np.stack([cx, sx]), np.stack([-sx, cx])])
    wxi = np.einsum("qrxdl,yt->rxtldyq", bx.reshape(2, 2, width_x, SLABS, 2), eye_y)
    wxi = wxi.reshape(256, 256)
    fy = np.stack([np.stack([cy, -sy]), np.stack([sy, cy])])
    ty = np.einsum("rqym,e->yrqem", fy, np.ones(4)).reshape(128, 256)
    by = np.stack([np.stack([cy, sy]), np.stack([-sy, cy])])
    tyi = np.einsum("rqym,ie->iyqrem", by, np.eye(4)).reshape(512, 256)
    tyr = np.einsum("rqym,e->yqrem", by, np.ones(4)).reshape(128, 256)
    zi8 = np.einsum("ab,rzk->rakbz", np.eye(8), fz).reshape(256, 8 * width_z)
    pick = np.stack([np.ones(1), np.zeros(1)]).reshape(2)
    zi4 = np.einsum("ab,rzk,e->raekbz", np.eye(4), fz, pick).reshape(256, 4 * width_z)
    zi8 = np.concatenate(np.split(zi8, 4, axis=1))
    zi4 = np.concatenate(np.split(zi4, 2, axis=1))
    return split_table(np.concatenate([z8, wx, z4, ty, tyi, wxi, zi8, zi4, tyr]))


def halves(value):
    high = value.astype(BF16)
    return high, (value - high.astype(F32)).astype(BF16)


def product(left, right, form=((1,), (0,))):
    def one(a, b):
        return lax.dot_general(a, b, (form, ((), ())), preferred_element_type=F32)

    total = one(left[0], right[0])
    if left[1] is not None:
        total = total + one(left[1], right[0])
    if right[1] is not None:
        total = total + one(left[0], right[1])
    return total


def block_kernel(scale_fwd, scale_inv, *refs):
    sources, refs = refs[:4], refs[4:]
    mix, bias, act, gin, gspec, gsum, sf, point, dpre, modes, dmodes, spec, dspec, gmix = refs[:14]
    send, recv, sums, send_sem, recv_sem, sum_send, sum_recv, load_sem = refs[14:22]
    places = refs[22:]
    sig, tables, w, cot = places

    def table(name, first=0, count=None):
        start, rows = TABLES[name]
        rows = slice(start + first, start + first + (count or rows))
        return tables[0, rows], tables[1, rows]
    me = lax.axis_index("yslab")
    channels = 20
    lane = lax.broadcasted_iota(jnp.int32, (128, 128), 1)

    def copy(step, chunk, peer):
        first, count = CHUNKS[chunk]
        return pltpu.make_async_remote_copy(
            src_ref=send.at[step, peer, pl.ds(first, count)],
            dst_ref=recv.at[step, me, pl.ds(first, count)],
            send_sem=send_sem.at[step, chunk, peer],
            recv_sem=recv_sem.at[step, chunk, me],
            device_id={"yslab": peer},
            device_id_type=pl.DeviceIdType.MESH,
        )

    def arrival(step, chunk, peer):
        first, count = CHUNKS[chunk]
        return pltpu.make_async_remote_copy(
            src_ref=send.at[step, peer, pl.ds(first, count)],
            dst_ref=recv.at[step, peer, pl.ds(first, count)],
            send_sem=send_sem.at[step, chunk, peer],
            recv_sem=recv_sem.at[step, chunk, peer],
            device_id={"yslab": peer},
            device_id_type=pl.DeviceIdType.MESH,
        )

    def sum_copy(peer, source):
        return pltpu.make_async_remote_copy(
            src_ref=sums.at[me],
            dst_ref=sums.at[source],
            send_sem=sum_send.at[peer],
            recv_sem=sum_recv.at[source],
            device_id={"yslab": peer},
            device_id_type=pl.DeviceIdType.MESH,
        )

    def each_peer(action):
        def body(i, carry):
            shift = 8 + lax.div(i, 2) * (1 - 2 * lax.rem(i, 2))
            action(lax.rem(me + shift, SLABS))
            return carry

        lax.fori_loop(1, SLABS, body, 0)

    def send_chunk(step, chunk):
        each_peer(lambda peer: copy(step, chunk, peer).start())
        first, count = CHUNKS[chunk]
        recv[step, pl.ds(me, 1), first:first + count] = send[step, pl.ds(me, 1), first:first + count]

    def wait_chunk(step, chunk):
        each_peer(lambda peer: arrival(step, chunk, peer).wait_recv())

    def forward_group(step, group, read, exact):
        name = "z8" if group < 2 else "z4"
        total = None
        for at in range(0, len(CHANS[group]), 2):
            pair = jnp.concatenate([read(c) for c in CHANS[group][at:at + 2]], axis=1)
            left = (pair, None) if exact else halves(pair)
            part = product(left, table(name, at * 128, 256))
            total = part if total is None else total + part
        stacked = jnp.concatenate([total[:, :128], total[:, 128:]], axis=0)
        out = product(table("wx"), halves(stacked))
        if group < 2:
            for jl in range(2):
                send[step, :, 2 * group + jl] = out[jl * 128:(jl + 1) * 128].reshape(16, 8, 128)
        else:
            send[step, :, 4] = jnp.where(lane < 64, out[:128], out[128:]).reshape(16, 8, 128)
        send_chunk(step, group)

    def spectra(step, group, target, scale):
        for jl in range(2 if group < 2 else 1):
            tile = recv[step, :, 2 * group + jl].reshape(128, 128) * scale
            out = product(halves(tile.T), table("ty"))
            if group < 2:
                for place, c in enumerate(CHANS[group]):
                    target[jl, c] = out[place * 16:(place + 1) * 16]
            else:
                for jj in range(2):
                    for place, c in enumerate(CHANS[2]):
                        row = jj * 64 + place * 16
                        target[jj, c] = out[row:row + 16]

    def back_group(step, group, use):
        if group < 2:
            one = recv[step, :, 2 * group].reshape(128, 128)
            two = recv[step, :, 2 * group + 1].reshape(128, 128)
            top = jnp.where(lane < 64, one, pltpu.roll(two, 64, 1))
            low = jnp.where(lane < 64, pltpu.roll(one, 64, 1), two)
        else:
            top = recv[step, :, 4].reshape(128, 128)
            low = pltpu.roll(top, 112, 1)
        out = product(table("wxi"), halves(jnp.concatenate([top, low], axis=0)))
        left = halves(jnp.concatenate([out[:128], out[128:]], axis=1))
        name = "zi8" if group < 2 else "zi4"
        for at in range(0, len(CHANS[group]), 2):
            field = product(left, table(name, at * 128, 256))
            use(CHANS[group][at], field[:, :128])
            use(CHANS[group][at + 1], field[:, 128:])

    def pointwise(source, weight, start):
        def block(at, carry):
            rows = pl.ds(pl.multiple_of(lax.rem(at, 4) * 32, 32), 32)
            first = lax.div(at, 4) * 4
            totals = [jnp.full((32, 128), start(first + i), F32) for i in range(4)]
            for b in range(channels):
                value = source[b, rows]
                for i in range(4):
                    totals[i] = totals[i] + weight(first + i, b) * value
            for i in range(4):
                point[first + i, rows] = totals[i]
            return carry

        lax.fori_loop(0, 20, block, 0)

    def rows_of(first, last):
        return pl.ds(TABLES[first][0], TABLES[last][0] + TABLES[last][1] - TABLES[first][0])

    early, late = rows_of("z8", "z4"), rows_of("ty", "tyr")

    def load(index):
        source, place = sources[index % 4], places[index % 4]
        if index in (1, 5):
            rows = early if index == 1 else late
            source, place = source.at[:, rows], place.at[:, rows]
        return pltpu.make_async_copy(source, place, load_sem.at[index])

    def loaded(*indices):
        for index in indices:
            load(index).wait()

    for index in (0, 1, 2, 5, 3):
        load(index).start()

    barrier = pltpu.get_barrier_semaphore()

    def greet(peer):
        pl.semaphore_signal(barrier, inc=1, device_id={"yslab": peer},
                            device_id_type=pl.DeviceIdType.MESH)

    each_peer(greet)
    pl.semaphore_wait(barrier, SLABS - 1)

    loaded(0, 1)

    for group in range(3):
        forward_group(0, group, lambda c: sig[c], True)
    sf[...] = sig[...].astype(F32)
    pointwise(sf, lambda a, b: mix[b, a], lambda a: bias[a])
    loaded(2, 5, 3)

    mixed = [(jnp.zeros((16, 640), F32), jnp.zeros((16, 640), F32)) for jl in range(2)]
    for group in range(3):
        wait_chunk(0, group)
        spectra(0, group, modes, scale_fwd)
        for jl in range(2):
            rows = slice(jl * 16, jl * 16 + 16)

            def add(n, total):
                if group < 2:
                    c = lax.rem(n, 4) * 4 + 2 * group + lax.div(n, 4)
                else:
                    c = 16 + n
                real, imag = total
                wr = w[rows, pl.ds(pl.multiple_of(c * 640, 128), 640)].astype(F32)
                wi = w[rows, pl.ds(pl.multiple_of(c * 640 + 12800, 128), 640)].astype(F32)
                value = modes[jl, c]
                ur = jnp.concatenate([value[:, :128]] * 5, axis=1)
                ui = jnp.concatenate([value[:, 128:]] * 5, axis=1)
                return real + wr * ur - wi * ui, imag + wr * ui + wi * ur

            mixed[jl] = lax.fori_loop(0, len(CHANS[group]), add, mixed[jl])
    for jl in range(2):
        real, imag = mixed[jl]
        for oq in range(5):
            cols = slice(oq * 128, (oq + 1) * 128)
            if oq < 4:
                starts = [jl * 64 + oq * 16]
            else:
                starts = [128 + dup * 32 + jl * 16 for dup in range(4)]
            for row in starts:
                spec[row:row + 16, :128] = real[:, cols]
                spec[row:row + 16, 128:] = imag[:, cols]
    last = jnp.zeros((128, 128), F32)
    right = halves(spec[...] * scale_inv)
    for q in range(2):
        grid = product(table("tyi", q * 256, 256), right, ((1,), (1,)))
        for ii in range(2):
            part = grid[ii * 128:(ii + 1) * 128]
            send[1, :, 2 * q + ii] = part[:, :128].reshape(16, 8, 128)
            last = jnp.where(lane // 32 == 2 * q + ii, part[:, 128:], last)
        send_chunk(1, q)
    send[1, :, 4] = last.reshape(16, 8, 128)
    send_chunk(1, 2)

    def activate(o, field):
        value = field + point[o]
        root = math.sqrt(2.0 / math.pi)
        square = value * value
        t = jnp.tanh(root * value * (1.0 + 0.044715 * square))
        half = 0.5 * (1.0 + t)
        act[o] = (value * half).astype(BF16)
        slope = half + 0.5 * value * (1.0 - t * t) * root * (1.0 + 3 * 0.044715 * square)
        dpre[o] = cot[o].astype(F32) * slope

    for group in range(3):
        wait_chunk(1, group)
        back_group(1, group, activate)
        forward_group(2, group, lambda c: dpre[c], False)


    def reduce_rows(value):
        return jnp.sum(value, axis=0, keepdims=True)

    def pair_sums(c, carry):
        field = sf[c]
        for o in range(channels):
            gmix[c, o:o + 1] = reduce_rows(field * dpre[o])
        return carry

    gmix[...] = jnp.zeros_like(gmix)
    lax.fori_loop(0, channels, pair_sums, 0)
    for o in range(channels):
        gmix[channels, o:o + 1] = reduce_rows(dpre[o])
    flat = gmix[...].reshape(768, 128)
    line = lax.broadcasted_iota(jnp.int32, (8, 128), 0)
    ones = jnp.ones((8, 128), BF16)
    packed = jnp.zeros((8, 128), F32)
    for r in range(6):
        high, low = halves(flat[r * 128:(r + 1) * 128])
        value = product((ones, None), (high, low), ((1,), (1,)))
        packed = jnp.where(line == r, value, packed)
    sums[pl.ds(me, 1)] = (packed * scale_fwd).reshape(1, 8, 128)
    each_peer(lambda peer: sum_copy(peer, me).start())

    for group in range(3):
        wait_chunk(2, group)
        spectra(2, group, dmodes, scale_inv)

    lanes = lax.broadcasted_iota(jnp.int32, (16, 128), 1) // 32
    for jl in range(2):
        rows = slice(jl * 16, jl * 16 + 16)
        parts = []
        for ri in range(2):
            tiles = []
            for oq in range(5):
                tile = dmodes[jl, oq * 4, :, ri * 128:ri * 128 + 128]
                for i in range(1, 4):
                    other = dmodes[jl, oq * 4 + i, :, ri * 128:ri * 128 + 128]
                    tile = jnp.where(lanes == i, other, tile)
                tiles.append(tile)
            parts.append(jnp.concatenate(tiles, axis=1))
        dr, di = parts

        for c in range(channels):
            wr = w[rows, c * 640:c * 640 + 640].astype(F32)
            wi = w[rows, c * 640 + 12800:c * 640 + 13440].astype(F32)
            real = wr * dr + wi * di
            imag = wr * di - wi * dr
            if c < 16:
                row = (c % 4) * 128 + jl * 64 + (c // 4) * 16
            else:
                row = 512 + (c - 16) * 32 + jl * 16
            for ri, value in ((0, real), (1, imag)):
                folded = value[:, :128]
                for oq in range(1, 5):
                    folded = folded + value[:, oq * 128:(oq + 1) * 128]
                dspec[row:row + 16, ri * 128:ri * 128 + 128] = folded
    for t in range(5):
        grid = product(table("tyr"), halves(dspec[t * 128:(t + 1) * 128] * scale_fwd), ((1,), (1,)))
        send[3, :, t] = grid.reshape(16, 8, 128)
        if t == 1 or t == 3 or t == 4:
            send_chunk(3, t // 2)

    for jl in range(2):
        rows = slice(jl * 16, jl * 16 + 16)
        parts = []
        for ri in range(2):
            tiles = []
            for oq in range(5):
                tile = dmodes[jl, oq * 4, :, ri * 128:ri * 128 + 128]
                for i in range(1, 4):
                    other = dmodes[jl, oq * 4 + i, :, ri * 128:ri * 128 + 128]
                    tile = jnp.where(lanes == i, other, tile)
                tiles.append(tile)
            parts.append(jnp.concatenate(tiles, axis=1))
        dr, di = parts

        def outer(c, carry):
            value = modes[jl, c]
            ur = jnp.concatenate([value[:, :128]] * 5, axis=1)
            ui = jnp.concatenate([value[:, 128:]] * 5, axis=1)
            gspec[rows, pl.ds(pl.multiple_of(c * 640, 128), 640)] = ur * dr + ui * di
            gspec[rows, pl.ds(pl.multiple_of(c * 640 + 12800, 128), 640)] = ur * di - ui * dr
            return carry

        lax.fori_loop(0, channels, outer, 0)

    pointwise(dpre, lambda a, b: mix[a, b], lambda a: 0.0)
    each_peer(lambda peer: sum_copy(peer, peer).wait_recv())
    gsum[...] = jnp.sum(sums[...], axis=0)

    def finish(c, field):
        gin[c] = (field + point[c]).astype(BF16)

    for group in range(3):
        wait_chunk(3, group)
        back_group(3, group, finish)

    each_peer(lambda peer: sum_copy(peer, me).wait_send())
    for step in range(4):
        for group in range(3):
            each_peer(lambda peer: copy(step, group, peer).wait_send())


def write_kernel(*refs):
    sums, sources = refs[0], refs[1:4]
    outs, gmix, gbias, sems = refs[4:7], refs[7], refs[8], refs[9]
    copies = [pltpu.make_async_copy(sources[i], outs[i], sems.at[i]) for i in range(3)]
    for copy in copies:
        copy.start()
    packed = sums[...]
    for c in range(20):
        at = (c % 4) * 32
        gmix[c:c + 1, :] = packed[c // 4:c // 4 + 1, at:at + 20]
    gbias[...] = packed[5:6, :20]
    for copy in copies:
        copy.wait()


def per_device(signal, cotangent, spectral_weight, mix_weight, mix_bias):
    channels, width_x, rows_y, width_z = signal.shape
    slabs = lax.axis_size("yslab")
    if (channels, width_x, rows_y, width_z, slabs) != (20, 32, ROWS, 128, SLABS):
        return per_device_general(signal, cotangent, spectral_weight, mix_weight, mix_bias)
    length_y = rows_y * slabs
    scale_fwd = 1.0 / math.sqrt(width_x * length_y * width_z)
    scale_inv = 1.0 / math.sqrt(4 * MODES**3)
    flat = (channels, width_x * rows_y, width_z)
    packed = jnp.asarray(host_tables(width_x, length_y, width_z))
    sources = [signal.reshape(flat), packed, spectral_weight, cotangent.reshape(flat)]
    vmem = pl.BlockSpec(memory_space=pltpu.VMEM)
    smem = pl.BlockSpec(memory_space=pltpu.SMEM)
    hbm = pl.BlockSpec(memory_space=pltpu.HBM)
    wide = jax.ShapeDtypeStruct(spectral_weight.shape, F32)
    grid = jax.ShapeDtypeStruct(flat, BF16)
    act, gin, gspec, gsum = pl.pallas_call(
        partial(block_kernel, scale_fwd, scale_inv),
        out_shape=(grid, grid, wide, jax.ShapeDtypeStruct((8, 128), F32)),
        in_specs=[hbm] * 4 + [smem, smem],
        out_specs=(vmem, vmem, vmem, vmem),
        scratch_shapes=[
            pltpu.VMEM(flat, F32),
            pltpu.VMEM(flat, F32),
            pltpu.VMEM(flat, F32),
            pltpu.VMEM((2, 20, 16, 256), F32),
            pltpu.VMEM((2, 20, 16, 256), F32),
            pltpu.VMEM((256, 256), F32),
            pltpu.VMEM((640, 256), F32),
            pltpu.VMEM((24, 32, 128), F32),
            pltpu.VMEM((4, SLABS, 5, 8, 128), F32),
            pltpu.VMEM((4, SLABS, 5, 8, 128), F32),
            pltpu.VMEM((SLABS, 8, 128), F32),
            pltpu.SemaphoreType.DMA((4, 3, SLABS)),
            pltpu.SemaphoreType.DMA((4, 3, SLABS)),
            pltpu.SemaphoreType.DMA((SLABS,)),
            pltpu.SemaphoreType.DMA((SLABS,)),
            pltpu.SemaphoreType.DMA((6,)),
        ] + [pltpu.VMEM(x.shape, x.dtype) for x in sources],
        compiler_params=pltpu.CompilerParams(
            collective_id=0, has_side_effects=True, vmem_limit_bytes=30 * 1024 * 1024
        ),
    )(*sources, mix_weight, mix_bias)
    act, gin, gspec, gmix, gbias = pl.pallas_call(
        write_kernel,
        out_shape=(
            grid, grid, wide,
            jax.ShapeDtypeStruct((20, 20), F32), jax.ShapeDtypeStruct((1, 20), F32),
        ),
        in_specs=[vmem] * 4,
        out_specs=(hbm, hbm, hbm, vmem, vmem),
        scratch_shapes=[pltpu.SemaphoreType.DMA((3,))],
        compiler_params=pltpu.CompilerParams(vmem_limit_bytes=4 * 1024 * 1024),
    )(gsum, act, gin, gspec)
    return act.reshape(signal.shape), gin.reshape(signal.shape), gspec, gmix, gbias.reshape(20)


def solution(mesh):
    placed = (
        P(None, "groups", "yslab", None),
        P(None, "groups", "yslab", None),
        P("yslab", None),
        P(),
        P(),
    )
    return jax.shard_map(
        per_device,
        mesh=mesh,
        in_specs=placed,
        out_specs=(
            P(None, "groups", "yslab", None),
            P(None, "groups", "yslab", None),
            P("yslab", "groups"),
            P("groups", None),
            P("groups"),
        ),
        check_vma=False,
    )
```
